256 devices in a mesh: dp: 4 (over x), expert: 32 (over z, y), pair: 2 (over core).
Axes of the slice: x: 4, y: 4, z: 8, core: 2. Of those that a mesh axis runs over, the one named last changes fastest.
Arguments:
- tokens: bfloat16 [4, 768, 3584], P('dp', ('expert', 'pair')), may hold values from -6 to 6
- cotangent: bfloat16 [4, 768, 3584], P('dp', ('expert', 'pair')), may hold values from -6 to 6
- routes: int32 [4, 768, 8], P('dp', ('expert', 'pair')), may hold values from 0 to 63, all different within a row; in each aligned block of 12 rows (0 to 11, 12 to 23, ..., all dimensions but the last counted through in order) at most 3 rows name the same one
- route_weight: bfloat16 [4, 768, 8], P('dp', ('expert', 'pair')), may hold values from 0.019897461 to 0.5
- gate_weight: bfloat16 [64, 3584, 1536], P(('expert', 'pair'), None, 'dp'), may hold values from -6 to 6
- up_weight: bfloat16 [64, 3584, 1536], P(('expert', 'pair'), None, 'dp'), may hold values from -6 to 6
- down_weight: bfloat16 [64, 1536, 3584], P(('expert', 'pair'), 'dp'), may hold values from -6 to 6
Outputs:
- merged_gate: bfloat16 [32, 3584, 1536], P('expert', 'pair', 'dp')
- merged_up: bfloat16 [32, 3584, 1536], P('expert', 'pair', 'dp')
- merged_down: bfloat16 [32, 1536, 3584], P('expert', 'dp', 'pair')
The draws below stay inside these ranges and needn't reach their ends.
Inputs may be any that keep to these rules, and one draw needn't show every extreme that they name: `routes`: each row names 8 different experts and every expert is named somewhere. Among the 12 rows of one device and one micro-batch no expert is named more than 3 times, and in some such block an expert is named exactly 3 times.
All inputs are finite; a program needn't handle non-finite values.
Results may differ from the reference program's by a relative error of at most 0.015.
Values may be sent and summed in bfloat16 or wider, within the bound.
No kernel may reach another device: no remote copies, remote signals or barrier semaphores. Data moves between devices by JAX's collectives and lax.ppermute only.
A program may use at most 192 MiB of HBM per device.

```python
import math
import jax
import jax.numpy as jnp
import numpy as np
from jax import lax

D = 3584
TOP = 8
FF = 1536
TOK_DEV = 12
EXPERTS = 64
PAIRS = 32
CAP = 3
MICRO = 4
MB_TOKENS = 768


def level_of(stream_key, extent, split, low, high):
    def one(dim, shards_of):
        heights = jax.random.uniform(jax.random.fold_in(jax.random.fold_in(stream_key, 6), dim), (shards_of,), jnp.float32, low / len(split), high / len(split))
        return jnp.repeat(jnp.exp(heights), extent[dim] // shards_of).reshape((-1,) + (1,) * (len(extent) - dim - 1))

    gain = one(*split[0])
    for cut in split[1:]:
        gain = gain * one(*cut)
    return gain


def assign_block(key, own, number, rows, number_of, top, most, lean):
    sequence = jax.random.permutation(key, number_of)
    packed, ordinary = load_shares(number_of, rows * top, most, lean, True), load_shares(number_of, rows * top, most, lean, False)
    places = jnp.arange(number_of)

    def named(lengths, offset_by):
        used = int((lengths > 0).sum())
        fixed = max(1, used // 4)
        moved = fixed + (places - fixed + offset_by * (used - fixed)) % max(1, number_of - fixed)
        return jnp.zeros((number_of,), jnp.int32).at[sequence[jnp.where(places < fixed, places, moved)]].set(jnp.asarray(lengths, jnp.int32))

    lengths = jnp.where(number % 4 == 0, named(packed, number // 4), named(ordinary, number - number // 4 - 1))
    mixed = jax.random.permutation(jax.random.fold_in(own, 3), number_of)
    giver, taker = mixed[0:number_of // 2 * 2:2], mixed[1:number_of // 2 * 2:2]
    margin = jnp.minimum(lengths[giver] - 1, most - lengths[taker]) // 2
    margin = jnp.where((giver == sequence[0]) | (taker == sequence[0]) | (lengths[taker] == 0), 0, jnp.maximum(margin, 0))
    moved = jax.random.randint(jax.random.fold_in(own, 4), (number_of // 2,), 0, 1 << 20) % (margin + 1)
    lengths = lengths.at[giver].add(-moved).at[taker].add(moved)
    labels = jnp.searchsorted(jnp.cumsum(lengths), jnp.arange(rows * top), side="right").astype(jnp.int32)
    table = labels.reshape(top, rows).T
    table = table[jax.random.permutation(jax.random.fold_in(own, 1), rows)]
    offset_by = jax.random.randint(jax.random.fold_in(own, 2), (rows, 1), 0, top)
    return jnp.take_along_axis(table, (jnp.arange(top)[None, :] + offset_by) % top, axis=1)


def load_shares(amount, total, reach, skew, full):
    loads = [(1 << 20) // math.isqrt(rank ** skew) + 1 for rank in range(1, amount + 1)]
    largest = reach if full else min(reach, max(-(-total // amount), total * loads[0] // sum(loads)))
    least = 1 if total - largest >= amount - 1 else 0
    holding, rest = [largest] + [least] * (amount - 1), total - largest - least * (amount - 1)
    while rest > 0:
        movable = [i for i in range(1, amount) if holding[i] < largest] or [i for i in range(1, amount) if holding[i] < reach]
        whole, remaining = sum([loads[i] for i in movable]), rest
        for i in movable:
            extra = min(reach - holding[i], max(1, remaining * loads[i] // whole), rest)
            holding[i] = holding[i] + extra
            rest = rest - extra
    return np.array(holding)


def bell_draw(rng, shape, deviation, bound, pieces=(), kind=jnp.bfloat16):
    factor_of = level_of(rng, shape, pieces, -0.22, 0.18) if pieces else 1.0
    entries = jax.random.normal(rng, shape, jnp.float32) * deviation * factor_of
    return jnp.minimum(jnp.maximum(entries, -bound), bound).astype(kind)


def setup_inputs(seed: int = 0) -> dict:
    arg_keys = jax.random.split(jax.random.key(seed), 8)
    tokens = bell_draw(arg_keys[0], (MICRO, MB_TOKENS, D), 1.0, 6.0, ((0, 4), (1, 64)))
    cotangent = bell_draw(arg_keys[1], (MICRO, MB_TOKENS, D), 1.0, 6.0, ((0, 4), (1, 64)))
    routes_keys = jax.random.split(jax.random.fold_in(arg_keys[2], 1), MICRO * MB_TOKENS // TOK_DEV)
    routes_turns = jax.random.permutation(jax.random.fold_in(arg_keys[2], 3), MICRO * MB_TOKENS // TOK_DEV)
    routes = jax.vmap(lambda own, number: assign_block(jax.random.fold_in(arg_keys[2], 2), own, number, TOK_DEV, EXPERTS, TOP, CAP, 2))(routes_keys, routes_turns).reshape((MICRO, MB_TOKENS, TOP))
    route_weight = jnp.clip(jnp.exp(math.log(0.5) - 3.224016 * jax.random.uniform(arg_keys[3], (MICRO, MB_TOKENS, TOP), jnp.float32) ** level_of(arg_keys[3], (MICRO, MB_TOKENS, TOP), ((0, 4), (1, 64)), -0.2, 0.2)), 0.019897461, 0.5).astype(jnp.bfloat16)
    gate_weight = bell_draw(arg_keys[4], (EXPERTS, D, FF), 1.0, 6.0, ((0, 64), (2, 4)))
    up_weight = bell_draw(arg_keys[5], (EXPERTS, D, FF), 1.0, 6.0, ((0, 64), (2, 4)))
    down_weight = bell_draw(arg_keys[6], (EXPERTS, FF, D), 1.0, 6.0, ((0, 64), (1, 4)))
    return dict(tokens=tokens, cotangent=cotangent, routes=routes, route_weight=route_weight, gate_weight=gate_weight, up_weight=up_weight, down_weight=down_weight)


FISHER_EPS = 1e-6
PRIOR_SHIFT = 0.1


def expert_fisher(x_in, c_in, gate_w, up_w, down_w):
    model_scale = D ** -0.5
    hidden_scale = FF ** -0.5
    fisher_gate = jnp.zeros((D, FF), jnp.float32)
    fisher_up = jnp.zeros((D, FF), jnp.float32)
    fisher_down = jnp.zeros((FF, D), jnp.float32)
    for micro in range(MICRO):
        rows_x = x_in[micro]
        rows_c = c_in[micro]
        pre_gate = jnp.dot(rows_x, gate_w, preferred_element_type=jnp.float32) * model_scale
        pre_up = jnp.dot(rows_x, up_w, preferred_element_type=jnp.float32) * model_scale
        sigmoid_gate = jax.nn.sigmoid(pre_gate)
        activated = pre_gate * sigmoid_gate
        hidden_state = (activated * pre_up).astype(jnp.bfloat16)
        d_hidden = jnp.dot(rows_c, down_w.T, preferred_element_type=jnp.float32) * hidden_scale
        slope = sigmoid_gate * (1.0 + pre_gate * (1.0 - sigmoid_gate))
        gate_gradient = (d_hidden * pre_up * slope).astype(jnp.bfloat16)
        up_gradient = (d_hidden * activated).astype(jnp.bfloat16)
        grad_gate = jnp.dot(rows_x.T, gate_gradient, preferred_element_type=jnp.float32) * model_scale
        grad_up = jnp.dot(rows_x.T, up_gradient, preferred_element_type=jnp.float32) * model_scale
        grad_down = jnp.dot(hidden_state.T, rows_c, preferred_element_type=jnp.float32) * hidden_scale
        fisher_gate = fisher_gate + grad_gate * grad_gate
        fisher_up = fisher_up + grad_up * grad_up
        fisher_down = fisher_down + grad_down * grad_down
    return fisher_gate, fisher_up, fisher_down


def weighted_terms(fisher, weight, axis):
    mean_value = jnp.mean(fisher, axis=axis, keepdims=True)
    shifted = fisher / (mean_value + FISHER_EPS) + PRIOR_SHIFT
    numer = (shifted * weight.astype(jnp.float32)).astype(jnp.bfloat16)
    denom = shifted.astype(jnp.bfloat16)
    return numer, denom


def combine_pair(first, second):
    first, second = lax.optimization_barrier((first, second))
    numer = first[0].astype(jnp.float32) + second[0].astype(jnp.float32)
    denom = first[1].astype(jnp.float32) + second[1].astype(jnp.float32)
    return (numer / denom).astype(jnp.bfloat16)


def reference(tokens, cotangent, routes, route_weight, gate_weight, up_weight, down_weight):
    tok_x = tokens.reshape(MICRO, EXPERTS, TOK_DEV, D).astype(jnp.float32)
    tok_c = cotangent.reshape(MICRO, EXPERTS, TOK_DEV, D).astype(jnp.float32)
    route_ids = routes.reshape(MICRO, EXPERTS, TOK_DEV, TOP)
    route_w = route_weight.reshape(MICRO, EXPERTS, TOK_DEV, TOP).astype(jnp.float32)
    onehot = (route_ids[..., None] == jnp.arange(EXPERTS, dtype=jnp.int32)).astype(jnp.float32)
    present = jnp.sum(onehot, axis=3)
    earlier = jnp.cumsum(present, axis=2) - present
    slot = jnp.einsum('mjtke,mjte->mjtk', onehot, earlier)
    slot_hot = (slot[..., None] == jnp.arange(CAP).astype(jnp.float32)).astype(jnp.float32)
    placed = jnp.einsum('mjtke,mjtks->emjst', onehot, slot_hot)
    weighted = jnp.einsum('mjtke,mjtks,mjtk->emjst', onehot, slot_hot, route_w)
    placed = placed.reshape(PAIRS, 2, MICRO, EXPERTS, CAP, TOK_DEV)
    weighted = weighted.reshape(PAIRS, 2, MICRO, EXPERTS, CAP, TOK_DEV)
    gate_pairs = gate_weight.reshape(PAIRS, 2, D, FF)
    up_pairs = up_weight.reshape(PAIRS, 2, D, FF)
    down_pairs = down_weight.reshape(PAIRS, 2, FF, D)

    def merge_one(inputs):
        placed_pair, weighted_pair, gate_pair, up_pair, down_pair = inputs
        terms = []
        for member in range(2):
            x_in = jnp.einsum('mjst,mjtd->mjsd', placed_pair[member], tok_x)
            x_in = x_in.astype(jnp.bfloat16).reshape(MICRO, EXPERTS * CAP, D)
            c_in = jnp.einsum('mjst,mjtd->mjsd', weighted_pair[member], tok_c)
            c_in = c_in.astype(jnp.bfloat16).reshape(MICRO, EXPERTS * CAP, D)
            fisher_gate, fisher_up, fisher_down = expert_fisher(x_in, c_in, gate_pair[member], up_pair[member], down_pair[member])
            terms.append((weighted_terms(fisher_gate, gate_pair[member], 0),
                          weighted_terms(fisher_up, up_pair[member], 0),
                          weighted_terms(fisher_down, down_pair[member], 1)))
        return (combine_pair(terms[0][0], terms[1][0]),
                combine_pair(terms[0][1], terms[1][1]),
                combine_pair(terms[0][2], terms[1][2]))

    merged_gate, merged_up, merged_down = lax.map(merge_one, (placed, weighted, gate_pairs, up_pairs, down_pairs))
    return merged_gate, merged_up, merged_down
```

```python
import jax
import jax.numpy as jnp
from jax import lax
from jax.sharding import PartitionSpec as P

D = 3584
HALF = 1792
FF = 1536
EXPERTS = 64
CAP = 3
TOK = 12
META = 128
FISHER_EPS = 1e-06
PRIOR_SHIFT = 0.1
BF = jnp.bfloat16
F32 = jnp.float32
Z, Y = 8, 4


def along_y(a, step):
    pairs = [(z * Y + y, z * Y + (y + step) % Y) for z in range(Z) for y in range(Y)]
    return lax.ppermute(a, "expert", pairs)


def along_z(a, step):
    pairs = [(z * Y + y, ((z + step) % Z) * Y + y) for z in range(Z) for y in range(Y)]
    return lax.ppermute(a, "expert", pairs)


def along_x(a, step):
    return lax.ppermute(a, "dp", [(i, (i + step) % 4) for i in range(4)])


def to_partner(a):
    return lax.ppermute(a, "pair", [(0, 1), (1, 0)])


def describe(routes, route_weight):
    onehot = (routes[:, :, None] == jnp.arange(EXPERTS, dtype=jnp.int32)).astype(F32)
    present = jnp.sum(onehot, axis=1)
    earlier = jnp.cumsum(present, axis=0) - present
    slot = jnp.sum(onehot * earlier[:, None, :], axis=2)
    meta = jnp.concatenate([routes.astype(BF), slot.astype(BF), route_weight], axis=1)
    return jnp.pad(meta, ((0, 0), (0, META - meta.shape[1])))


def spread_y(a):
    return jnp.concatenate([a, along_y(a, 1), along_y(a, -1), along_y(a, 2)], axis=1)


def place(block, experts):
    rows = block.shape[1]
    slots = rows // TOK * CAP
    meta = block[0, :, HALF:].astype(F32)
    ids, slot, weight = meta[:, :8], meta[:, 8:16], meta[:, 16:24]
    base = (jnp.arange(rows, dtype=jnp.int32) // TOK * CAP).astype(F32)[:, None]
    goal = jnp.arange(slots, dtype=jnp.int32).astype(F32)[None, :]
    picks, weighted = [], []
    for e in experts:
        mine = ids == e.astype(F32)
        target = jnp.sum(jnp.where(mine, slot + 1.0, 0.0), axis=1, keepdims=True)
        scale = jnp.sum(jnp.where(mine, weight, 0.0), axis=1, keepdims=True)
        hit = (target > 0.0) & (base + target - 1.0 == goal)
        picks.append(hit.astype(BF))
        weighted.append(jnp.where(hit, scale, 0.0).astype(BF))
    pick = jnp.concatenate(picks, axis=1)
    weigh = jnp.concatenate(weighted, axis=1)
    dims = (((0,), (0,)), ((), ()))
    slots_x = lax.dot_general(pick, block[0, :, :HALF], dims, preferred_element_type=F32)
    slots_c = lax.dot_general(weigh, block[1, :, :HALF], dims, preferred_element_type=F32)
    return jnp.stack([slots_x.astype(BF), slots_c.astype(BF)]).reshape(2, 2, slots, HALF)


def forward(rows, weights):
    gate_w, up_w, down_w = weights
    x, c = rows[0], rows[1]
    mine = jnp.stack([
        jnp.einsum("erd,edf->erf", x, gate_w, preferred_element_type=F32),
        jnp.einsum("erd,edf->erf", x, up_w, preferred_element_type=F32),
        jnp.einsum("erd,efd->erf", c, down_w, preferred_element_type=F32),
    ])
    other = to_partner(mine.astype(BF))
    total = mine + other[:, ::-1].astype(F32)
    pre_gate = total[0] * D ** (-0.5)
    pre_up = total[1] * D ** (-0.5)
    d_hidden = total[2] * FF ** (-0.5)
    sigmoid_gate = jax.nn.sigmoid(pre_gate)
    activated = pre_gate * sigmoid_gate
    hidden = (activated * pre_up).astype(BF)
    slope = sigmoid_gate * (1.0 + pre_gate * (1.0 - sigmoid_gate))
    d_gate = (d_hidden * pre_up * slope).astype(BF)
    d_up = (d_hidden * activated).astype(BF)
    return d_gate, d_up, hidden


def backward(rows, grads, batches):
    x, c = (r.reshape(2, batches, -1, HALF) for r in (rows[0], rows[1]))
    d_gate, d_up, hidden = (g.reshape(2, batches, -1, g.shape[-1]) for g in grads)
    out = []
    for left, right, scale in ((x, d_gate, 1.0 / D), (x, d_up, 1.0 / D), (hidden, c, 1.0 / FF)):
        total = 0.0
        for m in range(batches):
            g = jnp.einsum("erd,erf->edf", left[:, m], right[:, m], preferred_element_type=F32)
            total = total + g * g
        out.append(total * scale)
    return out


def local(tokens, cotangent, routes, route_weight, gate_weight, up_weight, down_weight):
    core = lax.axis_index("pair")
    pair = lax.axis_index("expert")
    experts = (2 * pair + core, 2 * pair + 1 - core)
    here, there = core * HALF, (1 - core) * HALF

    def half(a, axis, start):
        return lax.dynamic_slice_in_dim(a, start, HALF, axis)

    meta = describe(routes[0], route_weight[0])

    def packed(start):
        return jnp.stack([
            jnp.concatenate([half(tokens[0], 1, start), meta], axis=1),
            jnp.concatenate([half(cotangent[0], 1, start), meta], axis=1),
        ])

    kept, got = packed(here), to_partner(packed(there))
    own = jnp.concatenate(
        [jnp.where(core == 0, kept, got), jnp.where(core == 0, got, kept)], axis=1
    )
    opposite = along_x(own, 2)
    plane = spread_y(own)

    split = ((gate_weight[0], 0), (up_weight[0], 0), (down_weight[0], 1))
    weights = tuple(
        jnp.stack([half(w, axis, here), to_partner(half(w, axis, there))]) for w, axis in split
    )

    held = jnp.concatenate([plane, opposite], axis=1)
    up = down = held
    arrivals = [[held]]
    for _ in range(3):
        up, down = along_z(up, 1), along_z(down, -1)
        arrivals.append([up, down])
    arrivals.append([jnp.stack([along_z(up[0], 1), along_z(down[1], -1)])])
    groups = [arrivals[0] + arrivals[1], arrivals[2], arrivals[3] + arrivals[4]]

    wide = plane.shape[1]
    mine, before, after, across = [], [], [], []
    for group in groups:
        slots = place(jnp.concatenate([g[:, :wide] for g in group], axis=1), experts)
        mine.append(slots)
        before.append(along_x(slots, 1))
        after.append(along_x(slots, -1))
        raw = spread_y(jnp.concatenate([g[:, wide:] for g in group], axis=1))
        across.append(place(raw, experts))

    def whole(parts):
        return jnp.concatenate(parts, axis=2)

    fisher = None
    for batch in (mine, across, before, after):
        rows = whole(batch)
        sums = backward(rows, forward(rows, weights), 1)
        fisher = sums if fisher is None else [a + b for a, b in zip(fisher, sums)]

    part = jnp.stack([jnp.sum(fisher[0], 1), jnp.sum(fisher[1], 1), jnp.sum(fisher[2], 2)])
    mean = (part + to_partner(part)[:, ::-1]) * (1.0 / D)
    inverse = 1.0 / (mean + FISHER_EPS)

    outs = []
    for i in range(3):
        inv = inverse[i][:, None, :] if i < 2 else inverse[i][:, :, None]
        shifted = fisher[i] * inv + PRIOR_SHIFT
        numer = (shifted * weights[i].astype(F32)).astype(BF).astype(F32)
        denom = shifted.astype(BF).astype(F32)
        outs.append(((numer[0] + numer[1]) / (denom[0] + denom[1])).astype(BF)[None])
    return tuple(outs)


def solution(mesh):
    placed = (
        P("dp", ("expert", "pair"), None),
        P("dp", ("expert", "pair"), None),
        P("dp", ("expert", "pair"), None),
        P("dp", ("expert", "pair"), None),
        P(("expert", "pair"), None, "dp"),
        P(("expert", "pair"), None, "dp"),
        P(("expert", "pair"), "dp", None),
    )
    return jax.shard_map(
        local,
        mesh=mesh,
        in_specs=placed,
        out_specs=(P("expert", "pair", "dp"), P("expert", "pair", "dp"), P("expert", "dp", "pair")),
        check_vma=False,
    )
```

```python
import functools
import jax
import jax.numpy as jnp
from jax import lax
from jax.experimental import pallas as pl
from jax.experimental.pallas import tpu as pltpu
from jax.sharding import PartitionSpec as P

D = 3584
HALF = 1792
FF = 1536
EXPERTS = 64
CAP = 3
TOK = 12
META = 128
TILE = 256
FISHER_EPS = 1e-06
PRIOR_SHIFT = 0.1
BF = jnp.bfloat16
F32 = jnp.float32
Z, Y = 8, 4


def along_y(a, step):
    pairs = [(z * Y + y, z * Y + (y + step) % Y) for z in range(Z) for y in range(Y)]
    return lax.ppermute(a, "expert", pairs)


def along_z(a, step):
    pairs = [(z * Y + y, ((z + step) % Z) * Y + y) for z in range(Z) for y in range(Y)]
    return lax.ppermute(a, "expert", pairs)


def along_x(a, step):
    return lax.ppermute(a, "dp", [(i, (i + step) % 4) for i in range(4)])


def to_partner(a):
    return lax.ppermute(a, "pair", [(0, 1), (1, 0)])


def describe(routes, route_weight):
    onehot = (routes[:, :, None] == jnp.arange(EXPERTS, dtype=jnp.int32)).astype(F32)
    present = jnp.sum(onehot, axis=1)
    earlier = jnp.cumsum(present, axis=0) - present
    slot = jnp.sum(onehot * earlier[:, None, :], axis=2)
    meta = jnp.concatenate([routes.astype(BF), slot.astype(BF), route_weight], axis=1)
    return jnp.pad(meta, ((0, 0), (0, META - meta.shape[1])))


def place(block, experts):
    rows = block.shape[0]
    slots = -(-rows // (2 * TOK) * CAP // 16) * 16
    meta = block[:, HALF:].astype(F32)
    ids, slot, weight = meta[:, :8], meta[:, 8:16], meta[:, 16:24]
    row = jnp.arange(rows, dtype=jnp.int32)
    kind = (row // (2 * TOK) % 2)[:, None]
    source = row // (4 * TOK) * 2 + row % (2 * TOK) // TOK
    base = (source * CAP).astype(F32)[:, None]
    goal = jnp.arange(slots, dtype=jnp.int32).astype(F32)[None, :]
    picks = []
    for what in range(2):
        for e in experts:
            mine = ids == e.astype(F32)
            target = jnp.sum(jnp.where(mine, slot + 1.0, 0.0), axis=1, keepdims=True)
            hit = (target > 0.0) & (kind == what) & (base + target - 1.0 == goal)
            scale = jnp.sum(jnp.where(mine, weight, 0.0), axis=1, keepdims=True) if what else 1.0
            picks.append(jnp.where(hit, scale, 0.0).astype(BF))
    pick = jnp.concatenate(picks, axis=1)
    dims = (((0,), (0,)), ((), ()))
    placed = lax.dot_general(pick, block[:, :HALF], dims, preferred_element_type=F32)
    return placed.astype(BF).reshape(2, 2, slots, HALF)


def forward(rows, weights):
    up_weights, down_weights = weights
    wide = []
    for e in range(2):
        pre = jnp.dot(rows[0, e], up_weights[e], preferred_element_type=F32)
        back = lax.dot_general(
            rows[1, e], down_weights[e], (((1,), (1,)), ((), ())), preferred_element_type=F32
        )
        wide.append(jnp.concatenate([pre, back], axis=1))
    other = to_partner(jnp.stack([w.astype(BF) for w in wide]))
    part = down_weights[0].shape[0]
    both, hid = [], []
    for e in range(2):
        total = wide[e] + other[1 - e].astype(F32)
        pre_gate = total[:, :part] * D ** (-0.5)
        pre_up = total[:, part : 2 * part] * D ** (-0.5)
        d_hidden = total[:, 2 * part :] * FF ** (-0.5)
        sigmoid_gate = jax.nn.sigmoid(pre_gate)
        activated = pre_gate * sigmoid_gate
        slope = sigmoid_gate * (1.0 + pre_gate * (1.0 - sigmoid_gate))
        d_gate = (d_hidden * pre_up * slope).astype(BF)
        d_up = (d_hidden * activated).astype(BF)
        both.append(jnp.concatenate([d_gate, d_up], axis=1))
        hid.append((activated * pre_up).astype(BF))
    return jnp.stack(both), jnp.stack(hid)


def squares_kernel(recipe, carried, *refs):
    count = 1 + max(i for batch in recipe for i, _, _ in batch)
    rows, both, hid = refs[:count], refs[count : 2 * count], refs[2 * count : 3 * count]
    rest = refs[3 * count :]
    before, (fisher_in, fisher_out, sum_in, sum_out) = rest[: 4 * carried], rest[4 * carried :]
    dims = (((0,), (0,)), ((), ()))

    @pl.when(pl.program_id(0) == 0)
    def _():
        sum_in[...] = before[2][...] if carried else jnp.zeros_like(sum_in)
        sum_out[...] = before[3][...] if carried else jnp.zeros_like(sum_out)

    def cut(ref, batch, *lead):
        return jnp.concatenate([ref[i][(*lead, slice(a, b))] for i, a, b in batch], axis=0)

    for e in range(2):
        total_in = total_out = None
        for batch in recipe:
            x, c = cut(rows, batch, 0, e), cut(rows, batch, 1, e)
            d, h = cut(both, batch, e), cut(hid, batch, e)
            g = lax.dot_general(x, d, dims, preferred_element_type=F32)
            total_in = g * g if total_in is None else total_in + g * g
            g = lax.dot_general(h, c, dims, preferred_element_type=F32)
            total_out = g * g if total_out is None else total_out + g * g
        total_in = total_in * (1.0 / D)
        total_out = total_out * (1.0 / FF)
        sum_in[e] += jnp.sum(total_in, axis=0, keepdims=True)
        sum_out[e] += jnp.sum(total_out, axis=1, keepdims=True)
        if carried:
            total_in = total_in + before[0][e]
            total_out = total_out + before[1][e]
        fisher_in[e] = total_in
        fisher_out[e] = total_out


def squares(recipe, rows, grads, before=()):
    both, hid = [g[0] for g in grads], [g[1] for g in grads]
    part = hid[0].shape[-1]

    def all_of(shape):
        return pl.BlockSpec(shape, lambda i: (0,) * len(shape))

    state = [
        (jax.ShapeDtypeStruct((2, HALF, 2 * part), F32), pl.BlockSpec((2, TILE, 2 * part), lambda i: (0, i, 0))),
        (jax.ShapeDtypeStruct((2, part, HALF), F32), pl.BlockSpec((2, part, TILE), lambda i: (0, 0, i))),
        (jax.ShapeDtypeStruct((2, 1, 2 * part), F32), all_of((2, 1, 2 * part))),
        (jax.ShapeDtypeStruct((2, part, 1), F32), all_of((2, part, 1))),
    ]
    return pl.pallas_call(
        functools.partial(squares_kernel, recipe, int(bool(before))),
        grid=(HALF // TILE,),
        in_specs=[pl.BlockSpec((*r.shape[:3], TILE), lambda i: (0, 0, 0, i)) for r in rows]
        + [all_of(b.shape) for b in both]
        + [all_of(h.shape) for h in hid]
        + [spec for _, spec in state[: len(before)]],
        out_specs=[spec for _, spec in state],
        out_shape=[shape for shape, _ in state],
        compiler_params=pltpu.CompilerParams(vmem_limit_bytes=40 * 2**20),
    )(*rows, *both, *hid, *before)


def merge_kernel(
    core, fisher_in, fisher_out, scale_in, scale_out, *refs
):
    own, other, outs = refs[:3], refs[3:6], refs[6:]
    part = fisher_out.shape[1]
    for i in range(3):
        terms = []
        for e, weight in ((0, own[i]), (1, other[i])):
            if i < 2:
                cut = slice(i * part, (i + 1) * part)
                shifted = fisher_in[e, :, cut] * scale_in[e, :, cut] + PRIOR_SHIFT
            else:
                shifted = fisher_out[e] * scale_out[e] + PRIOR_SHIFT
            numer = (shifted * weight[...].reshape(shifted.shape).astype(F32)).astype(BF)
            terms.append((numer.astype(F32), shifted.astype(BF).astype(F32)))
        merged = (terms[0][0] + terms[1][0]) / (terms[0][1] + terms[1][1])
        outs[i][...] = merged.astype(BF).reshape(outs[i].shape)


def merge(core, fisher_in, fisher_out, scale_in, scale_out, own, other):
    steps = HALF // TILE
    part = fisher_out.shape[1]

    def all_of(shape):
        return pl.BlockSpec(shape, lambda i, c: (0,) * len(shape))

    tall, flat = (TILE, part), (part, TILE)
    return pl.pallas_call(
        merge_kernel,
        grid_spec=pltpu.PrefetchScalarGridSpec(
            num_scalar_prefetch=1,
            grid=(steps,),
            in_specs=[
                pl.BlockSpec((2, TILE, 2 * part), lambda i, c: (0, i, 0)),
                pl.BlockSpec((2, part, TILE), lambda i, c: (0, 0, i)),
                all_of(scale_in.shape),
                all_of(scale_out.shape),
                pl.BlockSpec((1, *tall), lambda i, c: (0, c[0] * steps + i, 0)),
                pl.BlockSpec((1, *tall), lambda i, c: (0, c[0] * steps + i, 0)),
                pl.BlockSpec((1, *flat), lambda i, c: (0, 0, c[0] * steps + i)),
                pl.BlockSpec(tall, lambda i, c: (i, 0)),
                pl.BlockSpec(tall, lambda i, c: (i, 0)),
                pl.BlockSpec(flat, lambda i, c: (0, i)),
            ],
            out_specs=[
                pl.BlockSpec((1, *tall), lambda i, c: (0, i, 0)),
                pl.BlockSpec((1, *tall), lambda i, c: (0, i, 0)),
                pl.BlockSpec((1, *flat), lambda i, c: (0, 0, i)),
            ],
        ),
        out_shape=[
            jax.ShapeDtypeStruct((1, HALF, part), BF),
            jax.ShapeDtypeStruct((1, HALF, part), BF),
            jax.ShapeDtypeStruct((1, part, HALF), BF),
        ],
        compiler_params=pltpu.CompilerParams(vmem_limit_bytes=40 * 2**20),
    )(core[None], fisher_in, fisher_out, scale_in, scale_out, *own, *other)


def local(tokens, cotangent, routes, route_weight, gate_weight, up_weight, down_weight):
    core = lax.axis_index("pair")
    pair = lax.axis_index("expert")
    experts = (2 * pair + core, 2 * pair + 1 - core)
    here, there = core * HALF, (1 - core) * HALF

    def half(a, axis, start):
        return lax.dynamic_slice_in_dim(a, start, HALF, axis)

    def rows_of(parts):
        return jnp.concatenate(parts, axis=2)

    meta = describe(routes[0], route_weight[0])

    def packed(start):
        return jnp.stack([
            jnp.concatenate([half(tokens[0], 1, start), meta], axis=1),
            jnp.concatenate([half(cotangent[0], 1, start), meta], axis=1),
        ])

    kept, got = packed(here), to_partner(packed(there))
    own = jnp.concatenate(
        [jnp.where(core == 0, kept, got), jnp.where(core == 0, got, kept)], axis=1
    ).reshape(4 * TOK, HALF + META)
    opposite = along_x(own, 2)
    plane = jnp.concatenate([own, along_y(own, 1), along_y(own, -1), along_y(own, 2)])
    far = lax.all_gather(opposite, "expert", axis=0, tiled=True)

    gate_weight, up_weight, down_weight, plane = lax.optimization_barrier(
        (gate_weight, up_weight, down_weight, plane)
    )
    split = ((gate_weight[0], 0), (up_weight[0], 0), (down_weight[0], 1))

    up1, down1 = along_z(plane, 1), along_z(plane, -1)
    up2, down2 = along_z(up1, 1), along_z(down1, -1)
    mine0 = place(jnp.concatenate([plane, up1, down1]), experts)
    prior0, next0 = along_x(mine0, 1), along_x(mine0, -1)
    up2, down2, mine0 = lax.optimization_barrier((up2, down2, mine0))
    up3, down3 = along_z(up2, 1), along_z(down2, -1)
    mine1 = place(jnp.concatenate([up2, down2]), experts)
    up3, down3, mine1, prior0, next0 = lax.optimization_barrier((up3, down3, mine1, prior0, next0))
    prior1, next1 = along_x(mine1, 1), along_x(mine1, -1)
    middle = plane.shape[0] // 2
    last = jnp.concatenate([along_z(up3[:middle], 1), along_z(down3[middle:], -1)])
    mine2 = place(jnp.concatenate([up3, down3, last]), experts)
    prior1, next1, mine2 = lax.optimization_barrier((prior1, next1, mine2))
    prior2, next2 = along_x(mine2, 1), along_x(mine2, -1)

    sent = [to_partner(half(w, axis, there)) for w, axis in split]
    stay = [half(w, axis, here) for w, axis in split]
    weights = (
        (jnp.concatenate(stay[:2], axis=1), jnp.concatenate(sent[:2], axis=1)),
        (stay[2], sent[2]),
    )

    mine = rows_of([mine0, mine1, mine2])
    mine_grads = forward(mine, weights)
    early = rows_of([prior0, prior1, next0, next1])
    early_grads = forward(early, weights)
    cuts = [0, up1.shape[0] * 3, up1.shape[0] * 5, up1.shape[0] * 8]
    across = rows_of([place(far[a:b], experts) for a, b in zip(cuts, cuts[1:])])
    across_grads = forward(across, weights)
    size = mine.shape[2]
    state = squares(
        (((0, 0, size),), ((1, 0, size),)), [mine, across], [mine_grads, across_grads]
    )
    late = rows_of([prior2, next2])
    late_grads = forward(late, weights)
    e, l = early.shape[2] // 2, late.shape[2] // 2
    recipe = (((0, 0, e), (1, 0, l)), ((0, e, 2 * e), (1, l, 2 * l)))
    fisher_in, fisher_out, sum_in, sum_out = squares(
        recipe, [early, late], [early_grads, late_grads], state
    )

    part = jnp.concatenate([sum_in[:, 0], sum_out[:, :, 0]], axis=1)
    mean = (part + to_partner(part)[::-1]) * (1.0 / D)
    inverse = 1.0 / (mean + FISHER_EPS)
    wide = sum_in.shape[2]
    return tuple(merge(
        core, fisher_in, fisher_out, inverse[:, None, :wide], inverse[:, wide:, None],
        (gate_weight, up_weight, down_weight), sent,
    ))


def solution(mesh):
    placed = (
        P("dp", ("expert", "pair"), None),
        P("dp", ("expert", "pair"), None),
        P("dp", ("expert", "pair"), None),
        P("dp", ("expert", "pair"), None),
        P(("expert", "pair"), None, "dp"),
        P(("expert", "pair"), None, "dp"),
        P(("expert", "pair"), "dp", None),
    )
    return jax.shard_map(
        local,
        mesh=mesh,
        in_specs=placed,
        out_specs=(P("expert", "pair", "dp"), P("expert", "pair", "dp"), P("expert", "dp", "pair")),
        check_vma=False,
    )
```

```python
import functools
import jax
import jax.numpy as jnp
from jax import lax
from jax.experimental import pallas as pl
from jax.experimental.pallas import tpu as pltpu
from jax.sharding import PartitionSpec as P

D = 3584
HALF = 1792
FF = 1536
EXPERTS = 64
CAP = 3
TOK = 12
META = 128
TILE = 256
FISHER_EPS = 1e-06
PRIOR_SHIFT = 0.1
BF = jnp.bfloat16
F32 = jnp.float32
Z, Y = 8, 4


def along_y(a, step):
    pairs = [(z * Y + y, z * Y + (y + step) % Y) for z in range(Z) for y in range(Y)]
    return lax.ppermute(a, "expert", pairs)


def along_z(a, step):
    pairs = [(z * Y + y, ((z + step) % Z) * Y + y) for z in range(Z) for y in range(Y)]
    return lax.ppermute(a, "expert", pairs)


def round_z(up, down, core):
    step = (1, -1)
    pairs = [
        ((z * Y + y) * 2 + c, (((z + step[c]) % Z) * Y + y) * 2 + c)
        for z in range(Z) for y in range(Y) for c in range(2)
    ]
    return lax.ppermute(jnp.where(core == 0, up, down), ("expert", "pair"), pairs)


def along_x(a, step):
    return lax.ppermute(a, "dp", [(i, (i + step) % 4) for i in range(4)])


def to_partner(a):
    return lax.ppermute(a, "pair", [(0, 1), (1, 0)])


def describe(routes, route_weight):
    onehot = (routes[:, :, None] == jnp.arange(EXPERTS, dtype=jnp.int32)).astype(F32)
    present = jnp.sum(onehot, axis=1)
    earlier = jnp.cumsum(present, axis=0) - present
    slot = jnp.sum(onehot * earlier[:, None, :], axis=2)
    meta = jnp.concatenate([routes.astype(BF), slot.astype(BF), route_weight], axis=1)
    return jnp.pad(meta, ((0, 0), (0, META - meta.shape[1])))


def place(block, experts):
    rows = block.shape[0]
    slots = rows // (2 * TOK) * CAP
    meta = block[:, HALF:].astype(F32)
    ids, slot, weight = meta[:, :8], meta[:, 8:16], meta[:, 16:24]
    row = jnp.arange(rows, dtype=jnp.int32)
    kind = (row // (2 * TOK) % 2)[:, None]
    source = row // (4 * TOK) * 2 + row % (2 * TOK) // TOK
    base = (source * CAP).astype(F32)[:, None]
    goal = jnp.arange(slots, dtype=jnp.int32).astype(F32)[None, :]
    picks = []
    for what in range(2):
        for e in experts:
            mine = ids == e.astype(F32)
            target = jnp.sum(jnp.where(mine, slot + 1.0, 0.0), axis=1, keepdims=True)
            hit = (target > 0.0) & (kind == what) & (base + target - 1.0 == goal)
            scale = jnp.sum(jnp.where(mine, weight, 0.0), axis=1, keepdims=True) if what else 1.0
            picks.append(jnp.where(hit, scale, 0.0).astype(BF))
    pick = jnp.concatenate(picks, axis=1)
    dims = (((0,), (0,)), ((), ()))
    placed = lax.dot_general(pick, block[:, :HALF], dims, preferred_element_type=F32)
    return placed.astype(BF).reshape(2, 2, slots, HALF)


def activate_kernel(*refs):
    pre, back, (more_pre, more_back, both, hid) = refs[:2], refs[2:4], refs[4:]
    part = back[0].shape[1]
    for e in range(2):
        total = pre[e][...] + more_pre[1 - e].astype(F32)
        pre_gate = total[:, :part] * D ** (-0.5)
        pre_up = total[:, part:] * D ** (-0.5)
        d_hidden = (back[e][...] + more_back[1 - e].astype(F32)) * FF ** (-0.5)
        sigmoid_gate = jax.nn.sigmoid(pre_gate)
        activated = pre_gate * sigmoid_gate
        slope = sigmoid_gate * (1.0 + pre_gate * (1.0 - sigmoid_gate))
        both[e, :, :part] = (d_hidden * pre_up * slope).astype(BF)
        both[e, :, part:] = (d_hidden * activated).astype(BF)
        hid[e] = (activated * pre_up).astype(BF)


def forward(rows, weights):
    up_weights, down_weights = weights
    pre = [jnp.dot(rows[0, e], up_weights[e], preferred_element_type=F32) for e in range(2)]
    back = [
        lax.dot_general(
            rows[1, e], down_weights[e], (((1,), (1,)), ((), ())), preferred_element_type=F32
        )
        for e in range(2)
    ]
    more_pre = to_partner(jnp.stack([a.astype(BF) for a in pre]))
    more_back = to_partner(jnp.stack([a.astype(BF) for a in back]))
    return pl.pallas_call(
        activate_kernel,
        out_shape=[
            jax.ShapeDtypeStruct(more_pre.shape, BF),
            jax.ShapeDtypeStruct(more_back.shape, BF),
        ],
        compiler_params=pltpu.CompilerParams(vmem_limit_bytes=16 * 2**20),
    )(*pre, *back, more_pre, more_back)


def squares_kernel(recipe, *refs):
    count = 1 + max(i for batch in recipe for i, _, _ in batch)
    rows, both, hid = refs[:count], refs[count : 2 * count], refs[2 * count : 3 * count]
    fisher_in, fisher_out, sum_in, sum_out = refs[3 * count :]
    dims = (((0,), (0,)), ((), ()))

    @pl.when(pl.program_id(0) == 0)
    def _():
        sum_in[...] = jnp.zeros_like(sum_in)
        sum_out[...] = jnp.zeros_like(sum_out)

    def cut(ref, batch, *lead):
        return jnp.concatenate([ref[i][(*lead, slice(a, b))] for i, a, b in batch], axis=0)

    for e in range(2):
        total_in = total_out = None
        for batch in recipe:
            x, c = cut(rows, batch, 0, e), cut(rows, batch, 1, e)
            d, h = cut(both, batch, e), cut(hid, batch, e)
            g = lax.dot_general(x, d, dims, preferred_element_type=F32)
            total_in = g * g if total_in is None else total_in + g * g
            g = lax.dot_general(h, c, dims, preferred_element_type=F32)
            total_out = g * g if total_out is None else total_out + g * g
        total_in = total_in * (1.0 / D)
        total_out = total_out * (1.0 / FF)
        sum_in[e] += jnp.sum(total_in, axis=0, keepdims=True)
        sum_out[e] += jnp.sum(total_out, axis=1, keepdims=True)
        fisher_in[e] = total_in.astype(BF)
        fisher_out[e] = total_out.astype(BF)


def squares(recipe, rows, grads):
    both, hid = [g[0] for g in grads], [g[1] for g in grads]
    part = hid[0].shape[-1]

    def all_of(shape):
        return pl.BlockSpec(shape, lambda i: (0,) * len(shape))

    state = [
        (jax.ShapeDtypeStruct((2, HALF, 2 * part), BF), pl.BlockSpec((2, TILE, 2 * part), lambda i: (0, i, 0))),
        (jax.ShapeDtypeStruct((2, part, HALF), BF), pl.BlockSpec((2, part, TILE), lambda i: (0, 0, i))),
        (jax.ShapeDtypeStruct((2, 1, 2 * part), F32), all_of((2, 1, 2 * part))),
        (jax.ShapeDtypeStruct((2, part, 1), F32), all_of((2, part, 1))),
    ]
    return pl.pallas_call(
        functools.partial(squares_kernel, recipe),
        grid=(HALF // TILE,),
        in_specs=[pl.BlockSpec((*r.shape[:3], TILE), lambda i: (0, 0, 0, i)) for r in rows]
        + [all_of(b.shape) for b in both]
        + [all_of(h.shape) for h in hid],
        out_specs=[spec for _, spec in state],
        out_shape=[shape for shape, _ in state],
        compiler_params=pltpu.CompilerParams(vmem_limit_bytes=24 * 2**20),
    )(*rows, *both, *hid)


def merge_kernel(
    core, fisher_in, fisher_out, sum_in, sum_out, more_in, more_out, *refs
):
    own, (wide, flat), outs = refs[:3], refs[3:5], refs[5:]
    part = fisher_out.shape[1]

    def scale(ours, theirs, e):
        return 1.0 / ((ours[e] + theirs[1 - e]) * (1.0 / D) + FISHER_EPS)

    scale_in = [scale(sum_in, more_in, e) for e in range(2)]
    scale_out = [scale(sum_out, more_out, e) for e in range(2)]
    for i in range(3):
        terms = []
        cut = slice(i * part, (i + 1) * part)
        for e in range(2):
            if i < 2:
                shifted = fisher_in[e, :, cut].astype(F32) * scale_in[e][:, cut] + PRIOR_SHIFT
                weight = own[i][0] if e == 0 else wide[:, cut]
            else:
                shifted = fisher_out[e].astype(F32) * scale_out[e] + PRIOR_SHIFT
                weight = own[i][0] if e == 0 else flat[...]
            terms.append((shifted * weight.astype(F32), shifted))
        merged = (terms[0][0] + terms[1][0]) / (terms[0][1] + terms[1][1])
        outs[i][0] = merged.astype(BF)


def merge(core, fisher_in, fisher_out, sums, own, other):
    steps = HALF // TILE
    part = fisher_out.shape[1]

    def all_of(shape):
        return pl.BlockSpec(shape, lambda i, c: (0,) * len(shape))

    tall, flat = (TILE, part), (part, TILE)
    return pl.pallas_call(
        merge_kernel,
        grid_spec=pltpu.PrefetchScalarGridSpec(
            num_scalar_prefetch=1,
            grid=(steps,),
            in_specs=[
                pl.BlockSpec((2, TILE, 2 * part), lambda i, c: (0, i, 0)),
                pl.BlockSpec((2, part, TILE), lambda i, c: (0, 0, i)),
                *(all_of(a.shape) for a in sums),
                pl.BlockSpec((1, *tall), lambda i, c: (0, c[0] * steps + i, 0)),
                pl.BlockSpec((1, *tall), lambda i, c: (0, c[0] * steps + i, 0)),
                pl.BlockSpec((1, *flat), lambda i, c: (0, 0, c[0] * steps + i)),
                pl.BlockSpec((TILE, 2 * part), lambda i, c: (i, 0)),
                pl.BlockSpec(flat, lambda i, c: (0, i)),
            ],
            out_specs=[
                pl.BlockSpec((1, *tall), lambda i, c: (0, i, 0)),
                pl.BlockSpec((1, *tall), lambda i, c: (0, i, 0)),
                pl.BlockSpec((1, *flat), lambda i, c: (0, 0, i)),
            ],
        ),
        out_shape=[
            jax.ShapeDtypeStruct((1, HALF, part), BF),
            jax.ShapeDtypeStruct((1, HALF, part), BF),
            jax.ShapeDtypeStruct((1, part, HALF), BF),
        ],
        compiler_params=pltpu.CompilerParams(vmem_limit_bytes=24 * 2**20),
    )(core[None], fisher_in, fisher_out, *sums, *own, *other)


def local(tokens, cotangent, routes, route_weight, gate_weight, up_weight, down_weight):
    core = lax.axis_index("pair")
    pair = lax.axis_index("expert")
    experts = (2 * pair + core, 2 * pair + 1 - core)
    here, there = core * HALF, (1 - core) * HALF

    def half(a, axis, start):
        return lax.dynamic_slice_in_dim(a, start, HALF, axis)

    def rows_of(parts):
        return jnp.concatenate(parts, axis=2)

    meta = describe(routes[0], route_weight[0])

    def packed(start):
        return jnp.stack([
            jnp.concatenate([half(tokens[0], 1, start), meta], axis=1),
            jnp.concatenate([half(cotangent[0], 1, start), meta], axis=1),
        ])

    kept, got = packed(here), to_partner(packed(there))
    own = jnp.concatenate(
        [jnp.where(core == 0, kept, got), jnp.where(core == 0, got, kept)], axis=1
    ).reshape(4 * TOK, HALF + META)
    held = jnp.concatenate([own, along_y(own, 1), along_y(own, -1), along_y(own, 2)])

    def onward(prior, following):
        return jnp.stack([along_x(prior[0], 1), along_x(following[1], -1)])

    def both_ways(slots):
        return along_x(slots, 1), along_x(slots, -1)

    tie = lax.optimization_barrier
    up1, down1 = along_z(held, 1), along_z(held, -1)
    mine0 = place(held, experts)
    up1, down1, mine0 = tie((up1, down1, mine0))
    up2, down2 = along_z(up1, 1), along_z(down1, -1)
    sides0 = both_ways(mine0)
    mine1 = place(jnp.concatenate([up1, down1]), experts)
    up2, down2, mine1, sides0 = tie((up2, down2, mine1, sides0))
    up3, down3 = along_z(up2, 1), along_z(down2, -1)
    sides1 = both_ways(mine1)
    mine2 = place(jnp.concatenate([up2, down2]), experts)
    up3, down3, mine2, sides1, gate_weight, up_weight, down_weight = tie(
        (up3, down3, mine2, sides1, gate_weight, up_weight, down_weight)
    )
    last = round_z(up3, down3, core)
    sides2 = both_ways(mine2)
    far1 = onward(*(rows_of([a, b]) for a, b in zip(sides0, sides1)))
    mine3 = place(jnp.concatenate([up3, down3, last]), experts)
    sides2, mine3 = tie((sides2, mine3))
    sides3 = both_ways(mine3)
    far2 = onward(*sides2)
    far3 = onward(*sides3)

    stay_wide = jnp.concatenate([half(gate_weight[0], 0, here), half(up_weight[0], 0, here)], axis=1)
    sent_wide = to_partner(
        jnp.concatenate([half(gate_weight[0], 0, there), half(up_weight[0], 0, there)], axis=1)
    )
    sent_down = to_partner(half(down_weight[0], 1, there))
    weights = ((stay_wide, sent_wide), (half(down_weight[0], 1, here), sent_down))

    mine = rows_of([mine0, mine1, mine2, mine3])
    mine_grads = forward(mine, weights)
    sides = rows_of([part[i] for i in range(2) for part in (sides0, sides1, sides2, sides3)])
    side_grads = forward(sides, weights)
    far = rows_of([far1, far2, far3])
    far_grads = forward(far, weights)
    size = mine.shape[2]
    recipe = (((0, 0, size),), ((1, 0, size),), ((1, size, 2 * size),), ((2, 0, size),))
    fisher_in, fisher_out, sum_in, sum_out = squares(
        recipe, [mine, sides, far], [mine_grads, side_grads, far_grads]
    )
    return tuple(merge(
        core, fisher_in, fisher_out, (sum_in, sum_out, to_partner(sum_in), to_partner(sum_out)),
        (gate_weight, up_weight, down_weight), (sent_wide, sent_down),
    ))


def solution(mesh):
    placed = (
        P("dp", ("expert", "pair"), None),
        P("dp", ("expert", "pair"), None),
        P("dp", ("expert", "pair"), None),
        P("dp", ("expert", "pair"), None),
        P(("expert", "pair"), None, "dp"),
        P(("expert", "pair"), None, "dp"),
        P(("expert", "pair"), "dp", None),
    )
    return jax.shard_map(
        local,
        mesh=mesh,
        in_specs=placed,
        out_specs=(P("expert", "pair", "dp"), P("expert", "pair", "dp"), P("expert", "dp", "pair")),
        check_vma=False,
    )
```

```python
import functools
import jax
import jax.numpy as jnp
from jax import lax
from jax.experimental import pallas as pl
from jax.experimental.pallas import tpu as pltpu
from jax.sharding import PartitionSpec as P

D = 3584
HALF = 1792
FF = 1536
EXPERTS = 64
CAP = 3
TOK = 12
META = 128
TILE = 256
FISHER_EPS = 1e-06
PRIOR_SHIFT = 0.1
BF = jnp.bfloat16
F32 = jnp.float32
Z, Y = 8, 4


def along_y(a, step):
    pairs = [(z * Y + y, z * Y + (y + step) % Y) for z in range(Z) for y in range(Y)]
    return lax.ppermute(a, "expert", pairs)


def along_z(a, step):
    pairs = [(z * Y + y, ((z + step) % Z) * Y + y) for z in range(Z) for y in range(Y)]
    return lax.ppermute(a, "expert", pairs)


def round_z(up, down, core):
    step = (1, -1)
    pairs = [
        ((z * Y + y) * 2 + c, (((z + step[c]) % Z) * Y + y) * 2 + c)
        for z in range(Z) for y in range(Y) for c in range(2)
    ]
    return lax.ppermute(jnp.where(core == 0, up, down), ("expert", "pair"), pairs)


def along_x(a, step):
    return lax.ppermute(a, "dp", [(i, (i + step) % 4) for i in range(4)])


def to_partner(a):
    return lax.ppermute(a, "pair", [(0, 1), (1, 0)])


def describe(routes, route_weight):
    onehot = (routes[:, :, None] == jnp.arange(EXPERTS, dtype=jnp.int32)).astype(F32)
    present = jnp.sum(onehot, axis=1)
    earlier = jnp.cumsum(present, axis=0) - present
    slot = jnp.sum(onehot * earlier[:, None, :], axis=2)
    meta = jnp.concatenate([routes.astype(BF), slot.astype(BF), route_weight], axis=1)
    return jnp.pad(meta, ((0, 0), (0, META - meta.shape[1])))


def place(block, experts):
    rows = block.shape[0]
    slots = rows // (2 * TOK) * CAP
    meta = block[:, HALF:].astype(F32)
    ids, slot, weight = meta[:, :8], meta[:, 8:16], meta[:, 16:24]
    row = jnp.arange(rows, dtype=jnp.int32)
    kind = (row // (2 * TOK) % 2)[:, None]
    source = row // (4 * TOK) * 2 + row % (2 * TOK) // TOK
    base = (source * CAP).astype(F32)[:, None]
    goal = jnp.arange(slots, dtype=jnp.int32).astype(F32)[None, :]
    picks = []
    for what in range(2):
        for e in experts:
            mine = ids == e.astype(F32)
            target = jnp.sum(jnp.where(mine, slot + 1.0, 0.0), axis=1, keepdims=True)
            hit = (target > 0.0) & (kind == what) & (base + target - 1.0 == goal)
            scale = jnp.sum(jnp.where(mine, weight, 0.0), axis=1, keepdims=True) if what else 1.0
            picks.append(jnp.where(hit, scale, 0.0).astype(BF))
    pick = jnp.concatenate(picks, axis=1)
    dims = (((0,), (0,)), ((), ()))
    placed = lax.dot_general(pick, block[:, :HALF], dims, preferred_element_type=F32)
    return placed.astype(BF).reshape(2, 2, slots, HALF)


def activate_kernel(*refs):
    pre, back, (more_pre, more_back, both, hid) = refs[:2], refs[2:4], refs[4:]
    part = back[0].shape[1]
    for e in range(2):
        total = pre[e][...] + more_pre[1 - e].astype(F32)
        pre_gate = total[:, :part] * D ** (-0.5)
        pre_up = total[:, part:] * D ** (-0.5)
        d_hidden = (back[e][...] + more_back[1 - e].astype(F32)) * FF ** (-0.5)
        sigmoid_gate = jax.nn.sigmoid(pre_gate)
        activated = pre_gate * sigmoid_gate
        slope = sigmoid_gate * (1.0 + pre_gate * (1.0 - sigmoid_gate))
        both[e, :, :part] = (d_hidden * pre_up * slope).astype(BF)
        both[e, :, part:] = (d_hidden * activated).astype(BF)
        hid[e] = (activated * pre_up).astype(BF)


def forward(rows, weights):
    up_weights, down_weights = weights
    pre = [jnp.dot(rows[0, e], up_weights[e], preferred_element_type=F32) for e in range(2)]
    back = [
        lax.dot_general(
            rows[1, e], down_weights[e], (((1,), (1,)), ((), ())), preferred_element_type=F32
        )
        for e in range(2)
    ]
    more_pre = to_partner(jnp.stack([a.astype(BF) for a in pre]))
    more_back = to_partner(jnp.stack([a.astype(BF) for a in back]))
    return pl.pallas_call(
        activate_kernel,
        out_shape=[
            jax.ShapeDtypeStruct(more_pre.shape, BF),
            jax.ShapeDtypeStruct(more_back.shape, BF),
        ],
        compiler_params=pltpu.CompilerParams(vmem_limit_bytes=16 * 2**20),
    )(*pre, *back, more_pre, more_back)


def squares_kernel(recipe, *refs):
    count = 1 + max(i for batch in recipe for i, _, _ in batch)
    rows, both, hid = refs[:count], refs[count : 2 * count], refs[2 * count : 3 * count]
    fisher_in, fisher_out, sum_in, sum_out = refs[3 * count :]
    dims = (((0,), (0,)), ((), ()))

    @pl.when(pl.program_id(0) == 0)
    def _():
        sum_in[...] = jnp.zeros_like(sum_in)
        sum_out[...] = jnp.zeros_like(sum_out)

    def cut(ref, batch, *lead):
        return jnp.concatenate([ref[i][(*lead, slice(a, b))] for i, a, b in batch], axis=0)

    for e in range(2):
        total_in = total_out = None
        for batch in recipe:
            x, c = cut(rows, batch, 0, e), cut(rows, batch, 1, e)
            d, h = cut(both, batch, e), cut(hid, batch, e)
            g = lax.dot_general(x, d, dims, preferred_element_type=F32)
            total_in = g * g if total_in is None else total_in + g * g
            g = lax.dot_general(h, c, dims, preferred_element_type=F32)
            total_out = g * g if total_out is None else total_out + g * g
        total_in = total_in * (1.0 / D)
        total_out = total_out * (1.0 / FF)
        sum_in[e] += jnp.sum(total_in, axis=0, keepdims=True)
        sum_out[e] += jnp.sum(total_out, axis=1, keepdims=True)
        fisher_in[e] = total_in.astype(BF)
        fisher_out[e] = total_out.astype(BF)


def squares(recipe, rows, grads):
    both, hid = [g[0] for g in grads], [g[1] for g in grads]
    part = hid[0].shape[-1]

    def all_of(shape):
        return pl.BlockSpec(shape, lambda i: (0,) * len(shape))

    state = [
        (jax.ShapeDtypeStruct((2, HALF, 2 * part), BF), pl.BlockSpec((2, TILE, 2 * part), lambda i: (0, i, 0))),
        (jax.ShapeDtypeStruct((2, part, HALF), BF), pl.BlockSpec((2, part, TILE), lambda i: (0, 0, i))),
        (jax.ShapeDtypeStruct((2, 1, 2 * part), F32), all_of((2, 1, 2 * part))),
        (jax.ShapeDtypeStruct((2, part, 1), F32), all_of((2, part, 1))),
    ]
    return pl.pallas_call(
        functools.partial(squares_kernel, recipe),
        grid=(HALF // TILE,),
        in_specs=[pl.BlockSpec((*r.shape[:3], TILE), lambda i: (0, 0, 0, i)) for r in rows]
        + [all_of(b.shape) for b in both]
        + [all_of(h.shape) for h in hid],
        out_specs=[spec for _, spec in state],
        out_shape=[shape for shape, _ in state],
        compiler_params=pltpu.CompilerParams(vmem_limit_bytes=20 * 2**20),
    )(*rows, *both, *hid)


def merge_kernel(
    core, fisher_in, fisher_out, sum_in, sum_out, more_in, more_out, *refs
):
    own, (wide, flat), outs = refs[:3], refs[3:5], refs[5:]
    part = fisher_out.shape[1]

    def scale(ours, theirs, e):
        return 1.0 / ((ours[e] + theirs[1 - e]) * (1.0 / D) + FISHER_EPS)

    scale_in = [scale(sum_in, more_in, e) for e in range(2)]
    scale_out = [scale(sum_out, more_out, e) for e in range(2)]
    for i in range(3):
        terms = []
        cut = slice(i * part, (i + 1) * part)
        for e in range(2):
            if i < 2:
                shifted = fisher_in[e, :, cut].astype(F32) * scale_in[e][:, cut] + PRIOR_SHIFT
                weight = own[i][0] if e == 0 else wide[:, cut]
            else:
                shifted = fisher_out[e].astype(F32) * scale_out[e] + PRIOR_SHIFT
                weight = own[i][0] if e == 0 else flat[...]
            terms.append((shifted * weight.astype(F32), shifted))
        merged = (terms[0][0] + terms[1][0]) / (terms[0][1] + terms[1][1])
        outs[i][0] = merged.astype(BF)


def merge(core, fisher_in, fisher_out, sums, own, other):
    steps = HALF // TILE
    part = fisher_out.shape[1]

    def all_of(shape):
        return pl.BlockSpec(shape, lambda i, c: (0,) * len(shape))

    tall, flat = (TILE, part), (part, TILE)
    return pl.pallas_call(
        merge_kernel,
        grid_spec=pltpu.PrefetchScalarGridSpec(
            num_scalar_prefetch=1,
            grid=(steps,),
            in_specs=[
                pl.BlockSpec((2, TILE, 2 * part), lambda i, c: (0, i, 0)),
                pl.BlockSpec((2, part, TILE), lambda i, c: (0, 0, i)),
                *(all_of(a.shape) for a in sums),
                pl.BlockSpec((1, *tall), lambda i, c: (0, c[0] * steps + i, 0)),
                pl.BlockSpec((1, *tall), lambda i, c: (0, c[0] * steps + i, 0)),
                pl.BlockSpec((1, *flat), lambda i, c: (0, 0, c[0] * steps + i)),
                pl.BlockSpec((TILE, 2 * part), lambda i, c: (i, 0)),
                pl.BlockSpec(flat, lambda i, c: (0, i)),
            ],
            out_specs=[
                pl.BlockSpec((1, *tall), lambda i, c: (0, i, 0)),
                pl.BlockSpec((1, *tall), lambda i, c: (0, i, 0)),
                pl.BlockSpec((1, *flat), lambda i, c: (0, 0, i)),
            ],
        ),
        out_shape=[
            jax.ShapeDtypeStruct((1, HALF, part), BF),
            jax.ShapeDtypeStruct((1, HALF, part), BF),
            jax.ShapeDtypeStruct((1, part, HALF), BF),
        ],
        compiler_params=pltpu.CompilerParams(vmem_limit_bytes=12 * 2**20),
    )(core[None], fisher_in, fisher_out, *sums, *own, *other)


def local(tokens, cotangent, routes, route_weight, gate_weight, up_weight, down_weight):
    core = lax.axis_index("pair")
    pair = lax.axis_index("expert")
    experts = (2 * pair + core, 2 * pair + 1 - core)
    here, there = core * HALF, (1 - core) * HALF

    def half(a, axis, start):
        return lax.dynamic_slice_in_dim(a, start, HALF, axis)

    def rows_of(parts):
        return jnp.concatenate(parts, axis=2)

    meta = describe(routes[0], route_weight[0])

    def packed(start):
        return jnp.stack([
            jnp.concatenate([half(tokens[0], 1, start), meta], axis=1),
            jnp.concatenate([half(cotangent[0], 1, start), meta], axis=1),
        ])

    kept, got = packed(here), to_partner(packed(there))
    own = jnp.concatenate(
        [jnp.where(core == 0, kept, got), jnp.where(core == 0, got, kept)], axis=1
    ).reshape(4 * TOK, HALF + META)
    held = jnp.concatenate([own, along_y(own, 1), along_y(own, -1), along_y(own, 2)])

    def onward(prior, following):
        return jnp.stack([along_x(prior[0], 1), along_x(following[1], -1)])

    def both_ways(slots):
        return along_x(slots, 1), along_x(slots, -1)

    tie = lax.optimization_barrier
    up1, down1 = along_z(held, 1), along_z(held, -1)
    mine0 = place(held, experts)
    sides0 = both_ways(mine0)
    up1, down1, sides0 = tie((up1, down1, sides0))
    up2, down2 = along_z(up1, 1), along_z(down1, -1)
    mine1 = place(jnp.concatenate([up1, down1]), experts)
    sides1 = both_ways(mine1)
    up2, down2, mine1 = tie((up2, down2, mine1))
    up3, down3 = along_z(up2, 1), along_z(down2, -1)
    mine2 = place(jnp.concatenate([up2, down2]), experts)
    sides2 = both_ways(mine2)
    up3, down3, mine2, sides1, gate_weight, up_weight, down_weight = tie(
        (up3, down3, mine2, sides1, gate_weight, up_weight, down_weight)
    )
    last = round_z(up3, down3, core)
    far1 = onward(*(rows_of([a, b]) for a, b in zip(sides0, sides1)))
    mine3 = place(jnp.concatenate([up3, down3]), experts)
    sides3 = both_ways(mine3)
    last, mine3, sides2 = tie((last, mine3, sides2))
    far2 = onward(*sides2)
    mine4 = place(last, experts)
    mine4, sides3, far1, far2 = tie((mine4, sides3, far1, far2))
    sides4 = both_ways(mine4)
    far3 = onward(*sides3)
    far4 = onward(*sides4)

    stay_wide = jnp.concatenate([half(gate_weight[0], 0, here), half(up_weight[0], 0, here)], axis=1)
    sent_wide = to_partner(
        jnp.concatenate([half(gate_weight[0], 0, there), half(up_weight[0], 0, there)], axis=1)
    )
    sent_down = to_partner(half(down_weight[0], 1, there))
    weights = ((stay_wide, sent_wide), (half(down_weight[0], 1, here), sent_down))

    mine = rows_of([mine0, mine1, mine2, mine3, mine4])
    mine_grads = forward(mine, weights)
    sides = rows_of([part[i] for i in range(2) for part in (sides0, sides1, sides2, sides3, sides4)])
    side_grads = forward(sides, weights)
    far = rows_of([far1, far2, far3, far4])
    far_grads = forward(far, weights)
    size = mine.shape[2]
    recipe = (((0, 0, size),), ((1, 0, size),), ((1, size, 2 * size),), ((2, 0, size),))
    fisher_in, fisher_out, sum_in, sum_out = squares(
        recipe, [mine, sides, far], [mine_grads, side_grads, far_grads]
    )
    return tuple(merge(
        core, fisher_in, fisher_out, (sum_in, sum_out, to_partner(sum_in), to_partner(sum_out)),
        (gate_weight, up_weight, down_weight), (sent_wide, sent_down),
    ))


def solution(mesh):
    placed = (
        P("dp", ("expert", "pair"), None),
        P("dp", ("expert", "pair"), None),
        P("dp", ("expert", "pair"), None),
        P("dp", ("expert", "pair"), None),
        P(("expert", "pair"), None, "dp"),
        P(("expert", "pair"), None, "dp"),
        P(("expert", "pair"), "dp", None),
    )
    return jax.shard_map(
        local,
        mesh=mesh,
        in_specs=placed,
        out_specs=(P("expert", "pair", "dp"), P("expert", "pair", "dp"), P("expert", "dp", "pair")),
        check_vma=False,
    )
```

```python
import functools
import jax
import jax.numpy as jnp
from jax import lax
from jax.experimental import pallas as pl
from jax.experimental.pallas import tpu as pltpu
from jax.sharding import PartitionSpec as P

D = 3584
HALF = 1792
FF = 1536
EXPERTS = 64
CAP = 3
TOK = 12
META = 128
TILE = 256
FISHER_EPS = 1e-06
PRIOR_SHIFT = 0.1
BF = jnp.bfloat16
F32 = jnp.float32
Z, Y = 8, 4


def along_y(a, step):
    pairs = [(z * Y + y, z * Y + (y + step) % Y) for z in range(Z) for y in range(Y)]
    return lax.ppermute(a, "expert", pairs)


def along_z(a, step):
    pairs = [(z * Y + y, ((z + step) % Z) * Y + y) for z in range(Z) for y in range(Y)]
    return lax.ppermute(a, "expert", pairs)


def round_z(up, down, core):
    step = (1, -1)
    pairs = [
        ((z * Y + y) * 2 + c, (((z + step[c]) % Z) * Y + y) * 2 + c)
        for z in range(Z) for y in range(Y) for c in range(2)
    ]
    return lax.ppermute(jnp.where(core == 0, up, down), ("expert", "pair"), pairs)


def along_x(a, step):
    return lax.ppermute(a, "dp", [(i, (i + step) % 4) for i in range(4)])


def to_partner(a):
    return lax.ppermute(a, "pair", [(0, 1), (1, 0)])


def describe(routes, route_weight):
    onehot = (routes[:, :, None] == jnp.arange(EXPERTS, dtype=jnp.int32)).astype(F32)
    present = jnp.sum(onehot, axis=1)
    earlier = jnp.cumsum(present, axis=0) - present
    slot = jnp.sum(onehot * earlier[:, None, :], axis=2)
    meta = jnp.concatenate([routes.astype(BF), slot.astype(BF), route_weight], axis=1)
    return jnp.pad(meta, ((0, 0), (0, META - meta.shape[1])))


def place(block, experts):
    rows = block.shape[0]
    slots = rows // (2 * TOK) * CAP
    meta = block[:, HALF:].astype(F32)
    ids, slot, weight = meta[:, :8], meta[:, 8:16], meta[:, 16:24]
    row = jnp.arange(rows, dtype=jnp.int32)
    kind = (row // (2 * TOK) % 2)[:, None]
    source = row // (4 * TOK) * 2 + row % (2 * TOK) // TOK
    base = (source * CAP).astype(F32)[:, None]
    goal = jnp.arange(slots, dtype=jnp.int32).astype(F32)[None, :]
    picks = []
    for what in range(2):
        for e in experts:
            mine = ids == e.astype(F32)
            target = jnp.sum(jnp.where(mine, slot + 1.0, 0.0), axis=1, keepdims=True)
            hit = (target > 0.0) & (kind == what) & (base + target - 1.0 == goal)
            scale = jnp.sum(jnp.where(mine, weight, 0.0), axis=1, keepdims=True) if what else 1.0
            picks.append(jnp.where(hit, scale, 0.0).astype(BF))
    pick = jnp.concatenate(picks, axis=1)
    dims = (((0,), (0,)), ((), ()))
    placed = lax.dot_general(pick, block[:, :HALF], dims, preferred_element_type=F32)
    return placed.astype(BF).reshape(2, 2, slots, HALF)


def activate_kernel(*refs):
    pre, back, (more_pre, more_back, both, hid) = refs[:2], refs[2:4], refs[4:]
    part = back[0].shape[1]
    for e in range(2):
        total = pre[e][...] + more_pre[1 - e].astype(F32)
        pre_gate = total[:, :part] * D ** (-0.5)
        pre_up = total[:, part:] * D ** (-0.5)
        d_hidden = (back[e][...] + more_back[1 - e].astype(F32)) * FF ** (-0.5)
        sigmoid_gate = jax.nn.sigmoid(pre_gate)
        activated = pre_gate * sigmoid_gate
        slope = sigmoid_gate * (1.0 + pre_gate * (1.0 - sigmoid_gate))
        both[e, :, :part] = (d_hidden * pre_up * slope).astype(BF)
        both[e, :, part:] = (d_hidden * activated).astype(BF)
        hid[e] = (activated * pre_up).astype(BF)


def forward(rows, weights):
    up_weights, down_weights = weights
    pre = [jnp.dot(rows[0, e], up_weights[e], preferred_element_type=F32) for e in range(2)]
    back = [
        lax.dot_general(
            rows[1, e], down_weights[e], (((1,), (1,)), ((), ())), preferred_element_type=F32
        )
        for e in range(2)
    ]
    more_pre = to_partner(jnp.stack([a.astype(BF) for a in pre]))
    more_back = to_partner(jnp.stack([a.astype(BF) for a in back]))
    return pl.pallas_call(
        activate_kernel,
        out_shape=[
            jax.ShapeDtypeStruct(more_pre.shape, BF),
            jax.ShapeDtypeStruct(more_back.shape, BF),
        ],
        compiler_params=pltpu.CompilerParams(vmem_limit_bytes=16 * 2**20),
    )(*pre, *back, more_pre, more_back)


def squares_kernel(recipe, *refs):
    count = 1 + max(i for batch in recipe for i, _, _ in batch)
    rows, both, hid = refs[:count], refs[count : 2 * count], refs[2 * count : 3 * count]
    fisher_in, fisher_out, sum_in, sum_out = refs[3 * count :]
    dims = (((0,), (0,)), ((), ()))

    @pl.when(pl.program_id(0) == 0)
    def _():
        sum_in[...] = jnp.zeros_like(sum_in)
        sum_out[...] = jnp.zeros_like(sum_out)

    def cut(ref, batch, *lead):
        return jnp.concatenate([ref[i][(*lead, slice(a, b))] for i, a, b in batch], axis=0)

    for e in range(2):
        total_in = total_out = None
        for batch in recipe:
            x, c = cut(rows, batch, 0, e), cut(rows, batch, 1, e)
            d, h = cut(both, batch, e), cut(hid, batch, e)
            g = lax.dot_general(x, d, dims, preferred_element_type=F32)
            total_in = g * g if total_in is None else total_in + g * g
            g = lax.dot_general(h, c, dims, preferred_element_type=F32)
            total_out = g * g if total_out is None else total_out + g * g
        total_in = total_in * (1.0 / D)
        total_out = total_out * (1.0 / FF)
        sum_in[e] += jnp.sum(total_in, axis=0, keepdims=True)
        sum_out[e] += jnp.sum(total_out, axis=1, keepdims=True)
        fisher_in[e] = total_in.astype(BF)
        fisher_out[e] = total_out.astype(BF)


def squares(recipe, rows, grads):
    both, hid = [g[0] for g in grads], [g[1] for g in grads]
    part = hid[0].shape[-1]

    def all_of(shape):
        return pl.BlockSpec(shape, lambda i: (0,) * len(shape))

    state = [
        (jax.ShapeDtypeStruct((2, HALF, 2 * part), BF), pl.BlockSpec((2, TILE, 2 * part), lambda i: (0, i, 0))),
        (jax.ShapeDtypeStruct((2, part, HALF), BF), pl.BlockSpec((2, part, TILE), lambda i: (0, 0, i))),
        (jax.ShapeDtypeStruct((2, 1, 2 * part), F32), all_of((2, 1, 2 * part))),
        (jax.ShapeDtypeStruct((2, part, 1), F32), all_of((2, part, 1))),
    ]
    return pl.pallas_call(
        functools.partial(squares_kernel, recipe),
        grid=(HALF // TILE,),
        in_specs=[pl.BlockSpec((*r.shape[:3], TILE), lambda i: (0, 0, 0, i)) for r in rows]
        + [all_of(b.shape) for b in both]
        + [all_of(h.shape) for h in hid],
        out_specs=[spec for _, spec in state],
        out_shape=[shape for shape, _ in state],
        compiler_params=pltpu.CompilerParams(vmem_limit_bytes=20 * 2**20),
    )(*rows, *both, *hid)


def merge_kernel(
    core, fisher_in, fisher_out, sum_in, sum_out, more_in, more_out, *refs
):
    own, (wide, flat), outs = refs[:3], refs[3:5], refs[5:]
    part = fisher_out.shape[1]

    def scale(ours, theirs, e):
        return 1.0 / ((ours[e] + theirs[1 - e]) * (1.0 / D) + FISHER_EPS)

    scale_in = [scale(sum_in, more_in, e) for e in range(2)]
    scale_out = [scale(sum_out, more_out, e) for e in range(2)]
    for i in range(3):
        terms = []
        cut = slice(i * part, (i + 1) * part)
        for e in range(2):
            if i < 2:
                shifted = fisher_in[e, :, cut].astype(F32) * scale_in[e][:, cut] + PRIOR_SHIFT
                weight = own[i][0] if e == 0 else wide[:, cut]
            else:
                shifted = fisher_out[e].astype(F32) * scale_out[e] + PRIOR_SHIFT
                weight = own[i][0] if e == 0 else flat[...]
            terms.append((shifted * weight.astype(F32), shifted))
        merged = (terms[0][0] + terms[1][0]) / (terms[0][1] + terms[1][1])
        outs[i][0] = merged.astype(BF)


def merge(core, fisher_in, fisher_out, sums, own, other):
    steps = HALF // TILE
    part = fisher_out.shape[1]

    def all_of(shape):
        return pl.BlockSpec(shape, lambda i, c: (0,) * len(shape))

    tall, flat = (TILE, part), (part, TILE)
    return pl.pallas_call(
        merge_kernel,
        grid_spec=pltpu.PrefetchScalarGridSpec(
            num_scalar_prefetch=1,
            grid=(steps,),
            in_specs=[
                pl.BlockSpec((2, TILE, 2 * part), lambda i, c: (0, i, 0)),
                pl.BlockSpec((2, part, TILE), lambda i, c: (0, 0, i)),
                *(all_of(a.shape) for a in sums),
                pl.BlockSpec((1, *tall), lambda i, c: (0, c[0] * steps + i, 0)),
                pl.BlockSpec((1, *tall), lambda i, c: (0, c[0] * steps + i, 0)),
                pl.BlockSpec((1, *flat), lambda i, c: (0, 0, c[0] * steps + i)),
                pl.BlockSpec((TILE, 2 * part), lambda i, c: (i, 0)),
                pl.BlockSpec(flat, lambda i, c: (0, i)),
            ],
            out_specs=[
                pl.BlockSpec((1, *tall), lambda i, c: (0, i, 0)),
                pl.BlockSpec((1, *tall), lambda i, c: (0, i, 0)),
                pl.BlockSpec((1, *flat), lambda i, c: (0, 0, i)),
            ],
        ),
        out_shape=[
            jax.ShapeDtypeStruct((1, HALF, part), BF),
            jax.ShapeDtypeStruct((1, HALF, part), BF),
            jax.ShapeDtypeStruct((1, part, HALF), BF),
        ],
        compiler_params=pltpu.CompilerParams(vmem_limit_bytes=12 * 2**20),
    )(core[None], fisher_in, fisher_out, *sums, *own, *other)


def local(tokens, cotangent, routes, route_weight, gate_weight, up_weight, down_weight):
    core = lax.axis_index("pair")
    pair = lax.axis_index("expert")
    experts = (2 * pair + core, 2 * pair + 1 - core)
    here, there = core * HALF, (1 - core) * HALF

    def half(a, axis, start):
        return lax.dynamic_slice_in_dim(a, start, HALF, axis)

    def rows_of(parts):
        return jnp.concatenate(parts, axis=2)

    meta = describe(routes[0], route_weight[0])

    def packed(start):
        return jnp.stack([
            jnp.concatenate([half(tokens[0], 1, start), meta], axis=1),
            jnp.concatenate([half(cotangent[0], 1, start), meta], axis=1),
        ])

    kept, got = packed(here), to_partner(packed(there))
    own = jnp.concatenate(
        [jnp.where(core == 0, kept, got), jnp.where(core == 0, got, kept)], axis=1
    ).reshape(4 * TOK, HALF + META)
    def spread(a):
        return jnp.concatenate([a, along_y(a, 1), along_y(a, -1), along_y(a, 2)])

    held = spread(own)

    def onward(prior, following):
        return jnp.stack([along_x(prior[0], 1), along_x(following[1], -1)])

    def both_ways(slots):
        return along_x(slots, 1), along_x(slots, -1)

    tie = lax.optimization_barrier
    up1, down1 = along_z(held, 1), along_z(held, -1)
    mine0 = place(held, experts)
    sides0 = both_ways(mine0)
    again, mine0 = tie((own, mine0))
    opposite = along_x(again, 2)
    up1, down1, sides0, opposite = tie((up1, down1, sides0, opposite))
    far_held = spread(opposite)
    up2, down2 = along_z(up1, 1), along_z(down1, -1)
    mine1 = place(jnp.concatenate([up1, down1]), experts)
    sides1 = both_ways(mine1)
    up2, down2, mine1 = tie((up2, down2, mine1))
    up3, down3 = along_z(up2, 1), along_z(down2, -1)
    mine2 = place(jnp.concatenate([up2, down2]), experts)
    sides2 = both_ways(mine2)
    up3, down3, mine2, sides1, far_held, gate_weight, up_weight, down_weight = tie(
        (up3, down3, mine2, sides1, far_held, gate_weight, up_weight, down_weight)
    )
    last = round_z(up3, down3, core)
    mine3 = place(jnp.concatenate([up3, down3]), experts)
    sides3 = both_ways(mine3)
    last, mine3, sides2, far_held = tie((last, mine3, sides2, far_held))
    far_up, far_down = along_z(far_held, 1), along_z(far_held, -1)
    mine4 = place(last, experts)
    mine4, sides3 = tie((mine4, sides3))
    sides4 = both_ways(mine4)
    far2 = onward(*(rows_of([a, b]) for a, b in zip(sides2, sides3)))
    sides4, far_up, far_down = tie((sides4, far_up, far_down))
    far3 = onward(*sides4)
    far1 = place(jnp.concatenate([far_held, far_up, far_down]), experts)

    stay_wide = jnp.concatenate([half(gate_weight[0], 0, here), half(up_weight[0], 0, here)], axis=1)
    sent_wide = to_partner(
        jnp.concatenate([half(gate_weight[0], 0, there), half(up_weight[0], 0, there)], axis=1)
    )
    sent_down = to_partner(half(down_weight[0], 1, there))
    weights = ((stay_wide, sent_wide), (half(down_weight[0], 1, here), sent_down))

    mine = rows_of([mine0, mine1, mine2, mine3, mine4])
    mine_grads = forward(mine, weights)
    sides = rows_of([part[i] for i in range(2) for part in (sides0, sides1, sides2, sides3, sides4)])
    side_grads = forward(sides, weights)
    far = rows_of([far1, far2, far3])
    far_grads = forward(far, weights)
    size = mine.shape[2]
    recipe = (((0, 0, size),), ((1, 0, size),), ((1, size, 2 * size),), ((2, 0, size),))
    fisher_in, fisher_out, sum_in, sum_out = squares(
        recipe, [mine, sides, far], [mine_grads, side_grads, far_grads]
    )
    return tuple(merge(
        core, fisher_in, fisher_out, (sum_in, sum_out, to_partner(sum_in), to_partner(sum_out)),
        (gate_weight, up_weight, down_weight), (sent_wide, sent_down),
    ))


def solution(mesh):
    placed = (
        P("dp", ("expert", "pair"), None),
        P("dp", ("expert", "pair"), None),
        P("dp", ("expert", "pair"), None),
        P("dp", ("expert", "pair"), None),
        P(("expert", "pair"), None, "dp"),
        P(("expert", "pair"), None, "dp"),
        P(("expert", "pair"), "dp", None),
    )
    return jax.shard_map(
        local,
        mesh=mesh,
        in_specs=placed,
        out_specs=(P("expert", "pair", "dp"), P("expert", "pair", "dp"), P("expert", "dp", "pair")),
        check_vma=False,
    )
```

```python
import functools
import jax
import jax.numpy as jnp
from jax import lax
from jax.experimental import pallas as pl
from jax.experimental.pallas import tpu as pltpu
from jax.sharding import PartitionSpec as P

D = 3584
HALF = 1792
FF = 1536
EXPERTS = 64
CAP = 3
TOK = 12
META = 128
TILE = 256
FISHER_EPS = 1e-06
PRIOR_SHIFT = 0.1
BF = jnp.bfloat16
F32 = jnp.float32
Z, Y = 8, 4


def along_y(a, step):
    pairs = [(z * Y + y, z * Y + (y + step) % Y) for z in range(Z) for y in range(Y)]
    return lax.ppermute(a, "expert", pairs)


def along_z(a, step):
    pairs = [(z * Y + y, ((z + step) % Z) * Y + y) for z in range(Z) for y in range(Y)]
    return lax.ppermute(a, "expert", pairs)


def round_z(up, down, core):
    step = (1, -1)
    pairs = [
        ((z * Y + y) * 2 + c, (((z + step[c]) % Z) * Y + y) * 2 + c)
        for z in range(Z) for y in range(Y) for c in range(2)
    ]
    return lax.ppermute(jnp.where(core == 0, up, down), ("expert", "pair"), pairs)


def along_x(a, step):
    return lax.ppermute(a, "dp", [(i, (i + step) % 4) for i in range(4)])


def to_partner(a):
    return lax.ppermute(a, "pair", [(0, 1), (1, 0)])


def describe(routes, route_weight):
    onehot = (routes[:, :, None] == jnp.arange(EXPERTS, dtype=jnp.int32)).astype(F32)
    present = jnp.sum(onehot, axis=1)
    earlier = jnp.cumsum(present, axis=0) - present
    slot = jnp.sum(onehot * earlier[:, None, :], axis=2)
    meta = jnp.concatenate([routes.astype(BF), slot.astype(BF), route_weight], axis=1)
    return jnp.pad(meta, ((0, 0), (0, META - meta.shape[1])))


def place(block, experts):
    rows = block.shape[0]
    slots = rows // (2 * TOK) * CAP
    meta = block[:, HALF:].astype(F32)
    ids, slot, weight = meta[:, :8], meta[:, 8:16], meta[:, 16:24]
    row = jnp.arange(rows, dtype=jnp.int32)
    kind = (row // (2 * TOK) % 2)[:, None]
    source = row // (4 * TOK) * 2 + row % (2 * TOK) // TOK
    base = (source * CAP).astype(F32)[:, None]
    goal = jnp.arange(slots, dtype=jnp.int32).astype(F32)[None, :]
    picks = []
    for what in range(2):
        for e in experts:
            mine = ids == e.astype(F32)
            target = jnp.sum(jnp.where(mine, slot + 1.0, 0.0), axis=1, keepdims=True)
            hit = (target > 0.0) & (kind == what) & (base + target - 1.0 == goal)
            scale = jnp.sum(jnp.where(mine, weight, 0.0), axis=1, keepdims=True) if what else 1.0
            picks.append(jnp.where(hit, scale, 0.0).astype(BF))
    pick = jnp.concatenate(picks, axis=1)
    dims = (((0,), (0,)), ((), ()))
    placed = lax.dot_general(pick, block[:, :HALF], dims, preferred_element_type=F32)
    return placed.astype(BF).reshape(2, 2, slots, HALF)


def activate_kernel(*refs):
    pre, back, (more_pre, more_back, both, hid) = refs[:2], refs[2:4], refs[4:]
    part = back[0].shape[1]
    for e in range(2):
        total = pre[e][...] + more_pre[1 - e].astype(F32)
        pre_gate = total[:, :part] * D ** (-0.5)
        pre_up = total[:, part:] * D ** (-0.5)
        d_hidden = (back[e][...] + more_back[1 - e].astype(F32)) * FF ** (-0.5)
        sigmoid_gate = jax.nn.sigmoid(pre_gate)
        activated = pre_gate * sigmoid_gate
        slope = sigmoid_gate * (1.0 + pre_gate * (1.0 - sigmoid_gate))
        both[e, :, :part] = (d_hidden * pre_up * slope).astype(BF)
        both[e, :, part:] = (d_hidden * activated).astype(BF)
        hid[e] = (activated * pre_up).astype(BF)


def project(rows, weights):
    up_weights, down_weights = weights
    pre = [jnp.dot(rows[0, e], up_weights[e], preferred_element_type=F32) for e in range(2)]
    back = [
        lax.dot_general(
            rows[1, e], down_weights[e], (((1,), (1,)), ((), ())), preferred_element_type=F32
        )
        for e in range(2)
    ]
    return pre, back


def activate(pre, back):
    more_pre = to_partner(jnp.stack([a.astype(BF) for a in pre]))
    more_back = to_partner(jnp.stack([a.astype(BF) for a in back]))
    return pl.pallas_call(
        activate_kernel,
        out_shape=[
            jax.ShapeDtypeStruct(more_pre.shape, BF),
            jax.ShapeDtypeStruct(more_back.shape, BF),
        ],
        compiler_params=pltpu.CompilerParams(vmem_limit_bytes=16 * 2**20),
    )(*pre, *back, more_pre, more_back)


def squares_kernel(recipe, *refs):
    count = 1 + max(i for batch in recipe for i, _, _ in batch)
    rows, both, hid = refs[:count], refs[count : 2 * count], refs[2 * count : 3 * count]
    fisher_in, fisher_out, sum_in, sum_out = refs[3 * count :]
    dims = (((0,), (0,)), ((), ()))

    @pl.when(pl.program_id(0) == 0)
    def _():
        sum_in[...] = jnp.zeros_like(sum_in)
        sum_out[...] = jnp.zeros_like(sum_out)

    def cut(ref, batch, *lead):
        return jnp.concatenate([ref[i][(*lead, slice(a, b))] for i, a, b in batch], axis=0)

    for e in range(2):
        total_in = total_out = None
        for batch in recipe:
            x, c = cut(rows, batch, 0, e), cut(rows, batch, 1, e)
            d, h = cut(both, batch, e), cut(hid, batch, e)
            g = lax.dot_general(x, d, dims, preferred_element_type=F32)
            total_in = g * g if total_in is None else total_in + g * g
            g = lax.dot_general(h, c, dims, preferred_element_type=F32)
            total_out = g * g if total_out is None else total_out + g * g
        total_in = total_in * (1.0 / D)
        total_out = total_out * (1.0 / FF)
        sum_in[e] += jnp.sum(total_in, axis=0, keepdims=True)
        sum_out[e] += jnp.sum(total_out, axis=1, keepdims=True)
        fisher_in[e] = total_in.astype(BF)
        fisher_out[e] = total_out.astype(BF)


def squares(recipe, rows, grads):
    both, hid = [g[0] for g in grads], [g[1] for g in grads]
    part = hid[0].shape[-1]

    def all_of(shape):
        return pl.BlockSpec(shape, lambda i: (0,) * len(shape))

    state = [
        (jax.ShapeDtypeStruct((2, HALF, 2 * part), BF), pl.BlockSpec((2, TILE, 2 * part), lambda i: (0, i, 0))),
        (jax.ShapeDtypeStruct((2, part, HALF), BF), pl.BlockSpec((2, part, TILE), lambda i: (0, 0, i))),
        (jax.ShapeDtypeStruct((2, 1, 2 * part), F32), all_of((2, 1, 2 * part))),
        (jax.ShapeDtypeStruct((2, part, 1), F32), all_of((2, part, 1))),
    ]
    return pl.pallas_call(
        functools.partial(squares_kernel, recipe),
        grid=(HALF // TILE,),
        in_specs=[pl.BlockSpec((*r.shape[:3], TILE), lambda i: (0, 0, 0, i)) for r in rows]
        + [all_of(b.shape) for b in both]
        + [all_of(h.shape) for h in hid],
        out_specs=[spec for _, spec in state],
        out_shape=[shape for shape, _ in state],
        compiler_params=pltpu.CompilerParams(vmem_limit_bytes=20 * 2**20),
    )(*rows, *both, *hid)


def merge_kernel(
    core, fisher_in, fisher_out, sum_in, sum_out, more_in, more_out, *refs
):
    own, (wide, flat), outs = refs[:3], refs[3:5], refs[5:]
    part = fisher_out.shape[1]

    def scale(ours, theirs, e):
        return 1.0 / ((ours[e] + theirs[1 - e]) * (1.0 / D) + FISHER_EPS)

    scale_in = [scale(sum_in, more_in, e) for e in range(2)]
    scale_out = [scale(sum_out, more_out, e) for e in range(2)]
    for i in range(3):
        terms = []
        cut = slice(i * part, (i + 1) * part)
        for e in range(2):
            if i < 2:
                shifted = fisher_in[e, :, cut].astype(F32) * scale_in[e][:, cut] + PRIOR_SHIFT
                weight = own[i][0] if e == 0 else wide[:, cut]
            else:
                shifted = fisher_out[e].astype(F32) * scale_out[e] + PRIOR_SHIFT
                weight = own[i][0] if e == 0 else flat[...]
            terms.append((shifted * weight.astype(F32), shifted))
        merged = (terms[0][0] + terms[1][0]) / (terms[0][1] + terms[1][1])
        outs[i][0] = merged.astype(BF)


def merge(core, fisher_in, fisher_out, sums, own, other):
    steps = HALF // TILE
    part = fisher_out.shape[1]

    def all_of(shape):
        return pl.BlockSpec(shape, lambda i, c: (0,) * len(shape))

    tall, flat = (TILE, part), (part, TILE)
    return pl.pallas_call(
        merge_kernel,
        grid_spec=pltpu.PrefetchScalarGridSpec(
            num_scalar_prefetch=1,
            grid=(steps,),
            in_specs=[
                pl.BlockSpec((2, TILE, 2 * part), lambda i, c: (0, i, 0)),
                pl.BlockSpec((2, part, TILE), lambda i, c: (0, 0, i)),
                *(all_of(a.shape) for a in sums),
                pl.BlockSpec((1, *tall), lambda i, c: (0, c[0] * steps + i, 0)),
                pl.BlockSpec((1, *tall), lambda i, c: (0, c[0] * steps + i, 0)),
                pl.BlockSpec((1, *flat), lambda i, c: (0, 0, c[0] * steps + i)),
                pl.BlockSpec((TILE, 2 * part), lambda i, c: (i, 0)),
                pl.BlockSpec(flat, lambda i, c: (0, i)),
            ],
            out_specs=[
                pl.BlockSpec((1, *tall), lambda i, c: (0, i, 0)),
                pl.BlockSpec((1, *tall), lambda i, c: (0, i, 0)),
                pl.BlockSpec((1, *flat), lambda i, c: (0, 0, i)),
            ],
        ),
        out_shape=[
            jax.ShapeDtypeStruct((1, HALF, part), BF),
            jax.ShapeDtypeStruct((1, HALF, part), BF),
            jax.ShapeDtypeStruct((1, part, HALF), BF),
        ],
        compiler_params=pltpu.CompilerParams(vmem_limit_bytes=12 * 2**20),
    )(core[None], fisher_in, fisher_out, *sums, *own, *other)


def local(tokens, cotangent, routes, route_weight, gate_weight, up_weight, down_weight):
    core = lax.axis_index("pair")
    pair = lax.axis_index("expert")
    experts = (2 * pair + core, 2 * pair + 1 - core)
    here, there = core * HALF, (1 - core) * HALF

    def half(a, axis, start):
        return lax.dynamic_slice_in_dim(a, start, HALF, axis)

    def rows_of(parts):
        return jnp.concatenate(parts, axis=2)

    meta = describe(routes[0], route_weight[0])

    def packed(start):
        return jnp.stack([
            jnp.concatenate([half(tokens[0], 1, start), meta], axis=1),
            jnp.concatenate([half(cotangent[0], 1, start), meta], axis=1),
        ])

    kept, got = packed(here), to_partner(packed(there))
    own = jnp.concatenate(
        [jnp.where(core == 0, kept, got), jnp.where(core == 0, got, kept)], axis=1
    ).reshape(4 * TOK, HALF + META)
    def spread(a):
        return jnp.concatenate([a, along_y(a, 1), along_y(a, -1), along_y(a, 2)])

    held = spread(own)

    def onward(prior, following):
        return jnp.stack([along_x(prior[0], 1), along_x(following[1], -1)])

    def both_ways(slots):
        return along_x(slots, 1), along_x(slots, -1)

    tie = lax.optimization_barrier
    up1, down1 = along_z(held, 1), along_z(held, -1)
    mine0 = place(held, experts)
    sides0 = both_ways(mine0)
    again, mine0 = tie((own, mine0))
    opposite = along_x(again, 2)
    up1, down1, sides0, opposite = tie((up1, down1, sides0, opposite))
    far_held = spread(opposite)
    up2, down2 = along_z(up1, 1), along_z(down1, -1)
    mine1 = place(jnp.concatenate([up1, down1]), experts)
    sides1 = both_ways(mine1)
    up2, down2, mine1 = tie((up2, down2, mine1))
    up3, down3 = along_z(up2, 1), along_z(down2, -1)
    mine2 = place(jnp.concatenate([up2, down2]), experts)
    sides2 = both_ways(mine2)
    up3, down3, mine2, sides1, far_held, gate_weight, up_weight, down_weight = tie(
        (up3, down3, mine2, sides1, far_held, gate_weight, up_weight, down_weight)
    )
    last = round_z(up3, down3, core)
    mine3 = place(jnp.concatenate([up3, down3]), experts)
    sides3 = both_ways(mine3)
    last, mine3, sides2, far_held = tie((last, mine3, sides2, far_held))
    far_up, far_down = along_z(far_held, 1), along_z(far_held, -1)
    mine4 = place(last, experts)
    mine4, sides3 = tie((mine4, sides3))
    sides4 = both_ways(mine4)
    far2 = onward(*(rows_of([a, b]) for a, b in zip(sides2, sides3)))
    sides4, far_up, far_down = tie((sides4, far_up, far_down))
    far3 = onward(*sides4)

    stay_wide = jnp.concatenate([half(gate_weight[0], 0, here), half(up_weight[0], 0, here)], axis=1)
    sent_wide = to_partner(
        jnp.concatenate([half(gate_weight[0], 0, there), half(up_weight[0], 0, there)], axis=1)
    )
    sent_down = to_partner(half(down_weight[0], 1, there))
    weights = ((stay_wide, sent_wide), (half(down_weight[0], 1, here), sent_down))

    mine = rows_of([mine0, mine1, mine2, mine3, mine4])
    mine_parts = project(mine, weights)
    sides = rows_of([part[i] for i in range(2) for part in (sides0, sides1, sides2, sides3, sides4)])
    side_parts = project(sides, weights)
    far_up, far_down, mine_parts, side_parts = tie((far_up, far_down, mine_parts, side_parts))
    far1 = place(jnp.concatenate([far_held, far_up, far_down]), experts)
    mine_grads = activate(*mine_parts)
    side_grads = activate(*side_parts)
    far = rows_of([far1, far2, far3])
    far_grads = activate(*project(far, weights))
    size = mine.shape[2]
    recipe = (((0, 0, size),), ((1, 0, size),), ((1, size, 2 * size),), ((2, 0, size),))
    fisher_in, fisher_out, sum_in, sum_out = squares(
        recipe, [mine, sides, far], [mine_grads, side_grads, far_grads]
    )
    return tuple(merge(
        core, fisher_in, fisher_out, (sum_in, sum_out, to_partner(sum_in), to_partner(sum_out)),
        (gate_weight, up_weight, down_weight), (sent_wide, sent_down),
    ))


def solution(mesh):
    placed = (
        P("dp", ("expert", "pair"), None),
        P("dp", ("expert", "pair"), None),
        P("dp", ("expert", "pair"), None),
        P("dp", ("expert", "pair"), None),
        P(("expert", "pair"), None, "dp"),
        P(("expert", "pair"), None, "dp"),
        P(("expert", "pair"), "dp", None),
    )
    return jax.shard_map(
        local,
        mesh=mesh,
        in_specs=placed,
        out_specs=(P("expert", "pair", "dp"), P("expert", "pair", "dp"), P("expert", "dp", "pair")),
        check_vma=False,
    )
```
